32 devices in a mesh: parts: 2 (over y), row: 4 (over z), col: 2 (over x), sub: 2 (over core).
Axes of the slice: x: 2, y: 2, z: 4, core: 2. Of those that a mesh axis runs over, the one named last changes fastest.
Arguments:
- tiles: float32 [128, 256, 256], P(('parts', 'row', 'col')), parts along dimension 0, may hold values from 0.01 to 1
- tile_rows: int32 [128], P(('parts', 'row', 'col')), parts along dimension 0, may hold values from 0 to 1, as said below
- tile_cols: int32 [128], P(('parts', 'row', 'col')), parts along dimension 0, may hold values from 0 to 3
- tile_counts: int32 [16], P(('parts', 'row', 'col')), parts along dimension 0, may hold values from 2 to 8
- start_panel: float32 [4096, 32], P(('parts', 'row', 'col'), 'sub'), parts along dimension 0, may hold values from -6 to 6
Outputs:
- lanczos_panel: float32 [4096, 32], P(('parts', 'row', 'col'), 'sub'), parts along dimension 0
- alphas: float32 [6, 32, 32], P('parts'), parts along dimension 0
- betas: float32 [8, 32, 32], P('parts'), parts along dimension 0
The draws below stay inside these ranges and needn't reach their ends.
There are 2 independent parts, one for each index of `parts`. The reference program is written for one: setup_inputs(seed, part) draws one part's arguments, and reference() takes and returns one part's arrays. A program takes and returns all parts, laid end to end along the dimension named above; each array names one. Nothing has to cross between parts.
Inputs may be any that keep to these rules, and one draw needn't show every extreme that they name: `tile_rows`: within one index pair of row and col, slots hold distinct pairs of row and column block.
All inputs are finite; a program needn't handle non-finite values.
Results may differ from the reference program's by a relative error of at most 0.0003.
Values sent between devices are 32-bit elements; how exact they have to be, the bound alone decides.
A program may use at most 64 MiB of HBM per device.

```python
import math
import jax
import jax.numpy as jnp
from jax import lax

TB = 256
PANEL = 32
ITERS = 3
BPD = 1
SLOTS = 8
NODES = 2048
N_ROW = 4
N_COL = 2


def tile_layout(key):
    devices_all = N_ROW * N_COL
    pairs = BPD * N_COL * BPD * N_ROW
    keys = jax.random.split(key, devices_all)
    picked = jax.vmap(lambda device_key: jax.random.permutation(device_key, pairs)[:SLOTS])(keys)
    return picked.reshape(-1).astype(jnp.int32)


def draw_tile_rows(key, part):
    picked = tile_layout(key)
    return (picked // (BPD * N_ROW)).astype(jnp.int32)


def draw_tile_cols(key, part):
    picked = tile_layout(key)
    return (picked % (BPD * N_ROW)).astype(jnp.int32)


def draw_tile_counts(key, part):
    key = jax.random.fold_in(key, 3)
    devices_all = N_ROW * N_COL
    first_key, second_key = jax.random.split(key)
    base_counts = jax.random.randint(first_key, (devices_all,), 2, SLOTS // 2 + 1)
    order = jax.random.permutation(second_key, devices_all)
    heavy = order < devices_all // 8
    return jnp.where(heavy, SLOTS, base_counts).astype(jnp.int32)


def shard_levels(key, dims, shards, smallest, top_value):
    loudness = 1.0
    for axis_at, blocks in shards:
        steps = jax.random.uniform(jax.random.fold_in(jax.random.fold_in(key, 6), axis_at), (blocks,), jnp.float32, smallest / len(shards), top_value / len(shards))
        loudness = loudness * jnp.repeat(jnp.exp(steps), dims[axis_at] // blocks).reshape((-1,) + (1,) * (len(dims) - 1 - axis_at))
    return loudness


def bell_draw(own_key, dims, scale, limit, cuts=(), kind=jnp.bfloat16):
    gain = shard_levels(own_key, dims, cuts, -0.22, 0.18) if cuts else 1.0
    drawn = jax.random.normal(own_key, dims, jnp.float32) * scale * gain
    return jnp.minimum(jnp.maximum(drawn, -limit), limit).astype(kind)


def setup_inputs(seed: int = 0, part: int = 0) -> dict:
    arg_keys = jax.random.split(jax.random.key(seed), 6)
    part_keys = jax.random.split(jax.random.fold_in(arg_keys[5], part), 6)
    return {
        "tiles": jnp.clip(jnp.exp(math.log(1.0) - 4.6051702 * jax.random.uniform(part_keys[0], (N_ROW * N_COL * SLOTS, TB, TB), jnp.float32) ** shard_levels(part_keys[0], (N_ROW * N_COL * SLOTS, TB, TB), ((0, 8),), -0.2, 0.2)), 0.01, 1.0),
        "tile_rows": draw_tile_rows(jax.random.fold_in(jax.random.fold_in(arg_keys[5], part), 71), part),
        "tile_cols": draw_tile_cols(jax.random.fold_in(jax.random.fold_in(arg_keys[5], part), 71), part),
        "tile_counts": draw_tile_counts(jax.random.fold_in(jax.random.fold_in(arg_keys[5], part), 71), part),
        "start_panel": bell_draw(part_keys[4], (NODES, PANEL), 1.0, 6.0, ((0, 8), (1, 2)), jnp.float32),
    }


def orthonormalize(panel):
    gram_matrix = jnp.dot(panel.T, panel, precision=lax.Precision.HIGHEST)
    factor = jnp.linalg.cholesky(gram_matrix)
    result = jax.scipy.linalg.solve_triangular(factor, panel.T, lower=True).T
    return (result, factor)

def reference(tiles, tile_rows, tile_cols, tile_counts, start_panel):
    devices_all = N_ROW * N_COL
    row_span = BPD * N_COL
    block_total = row_span * N_ROW
    position = jnp.arange(devices_all * SLOTS, dtype=jnp.int32)
    device = position // SLOTS
    active = (position % SLOTS < tile_counts[device]).astype(jnp.float32)
    row_block = device // N_COL * row_span + tile_rows
    col_block = tile_cols // BPD * row_span + device % N_COL * BPD + tile_cols % BPD
    row_sums = lax.optimization_barrier(jnp.sum(tiles, axis=2)) * active[:, None]
    degree = 1.0 + jnp.zeros((block_total, TB), jnp.float32).at[row_block].add(row_sums).reshape(-1)
    inv_root = (1.0 / jnp.sqrt(degree))[:, None]

    def operate(panel):
        blocks = (inv_root * panel).reshape(block_total, TB, PANEL)
        product = jnp.einsum('sab,sbc->sac', tiles, blocks[col_block], precision=lax.Precision.HIGHEST)
        product = product * active[:, None, None]
        summed = jnp.zeros((block_total, TB, PANEL), jnp.float32).at[row_block].add(product)
        return inv_root * summed.reshape(-1, PANEL)
    current, factor = orthonormalize(start_panel)
    betas = [factor.T]
    alphas = []
    previous = None
    for iteration in range(ITERS):
        residual = operate(current)
        if previous is not None:
            residual = residual - jnp.dot(previous, betas[-1].T, precision=lax.Precision.HIGHEST)
        alpha_block = jnp.dot(current.T, residual, precision=lax.Precision.HIGHEST)
        residual = residual - jnp.dot(current, alpha_block, precision=lax.Precision.HIGHEST)
        following, factor = orthonormalize(residual)
        alphas.append(alpha_block)
        betas.append(factor.T)
        previous, current = (current, following)
    return (current, jnp.stack(alphas), jnp.stack(betas))
```

```python
import functools

import jax
import jax.numpy as jnp
from jax import lax
from jax.experimental import pallas as pl
from jax.experimental.pallas import tpu as pltpu
from jax.sharding import PartitionSpec as P

ITERS = 3


def full_dot(left, right):
    return jnp.dot(left, right, precision=lax.Precision.HIGHEST)


def join_halves(half):
    return lax.all_gather(half, "sub", axis=1, tiled=True)


def factorize(gram_matrix, panel):
    factor = jnp.linalg.cholesky(gram_matrix)
    result = jax.scipy.linalg.solve_triangular(factor, panel.T, lower=True).T
    return (result, factor)


def tile_products(
    pooled_tiles, pooled_rows, pooled_cols, slot_of, first_index, end_index, blocks, row_total
):
    tile_side = pooled_tiles.shape[1]
    half_width = blocks.shape[2]
    per_turn = 4
    turn_count = (end_index - first_index + per_turn - 1) // per_turn

    def one_turn(position, summed):
        virtual = first_index + position * per_turn + jnp.arange(per_turn, dtype=jnp.int32)
        active = virtual < end_index
        clamped = jnp.clip(slot_of(virtual), 0, pooled_tiles.shape[0] - 1)
        chosen = jnp.take(pooled_tiles, clamped, axis=0)
        needed = jnp.take(blocks, jnp.take(pooled_cols, clamped), axis=0)
        product = jnp.einsum("gab,gbc->gac", chosen, needed, precision=lax.Precision.HIGHEST)
        targets = jnp.take(pooled_rows, clamped)
        select = (
            (targets[:, None] == jnp.arange(row_total, dtype=jnp.int32)[None, :]) & active[:, None]
        ).astype(jnp.float32)
        return summed + jnp.einsum("gr,gac->rac", select, product, precision=lax.Precision.HIGHEST)

    empty = jnp.zeros((row_total, tile_side, half_width), jnp.float32)
    return lax.fori_loop(0, turn_count, one_turn, empty)


def on_device(tiles, tile_rows, tile_cols, tile_counts, start_panel):
    slot_count = tiles.shape[0]
    tile_side = tiles.shape[1]
    local_rows = start_panel.shape[0]
    half_width = start_panel.shape[1]
    local_blocks = local_rows // tile_side
    row_span = local_blocks * lax.axis_size("col")
    my_count = tile_counts[0]
    side = lax.axis_index("sub")
    own_active = jnp.arange(slot_count, dtype=jnp.int32) < my_count
    in_use = own_active.astype(jnp.float32)
    row_sums = jnp.sum(tiles, axis=2)
    placing = (tile_rows[:, None] == jnp.arange(row_span, dtype=jnp.int32)[None, :]).astype(
        jnp.float32
    ) * in_use[:, None]
    partial_degree = full_dot(placing.T, row_sums).reshape(-1)
    degree = 1.0 + lax.psum_scatter(partial_degree, "col", scatter_dimension=0, tiled=True)
    inv_root = (1.0 / jnp.sqrt(degree))[:, None]

    def identity_slot(virtual):
        return virtual

    start_full = join_halves(start_panel)
    start_gram = lax.psum(full_dot(start_full.T, start_full), ("row", "col"))
    current, factor = factorize(start_gram, start_full)
    betas = [factor.T]
    alphas = []
    previous = None
    for iteration in range(ITERS):
        current_half = lax.dynamic_slice_in_dim(current, side * half_width, half_width, 1)
        scaled_half = inv_root * current_half
        gathered = lax.all_gather(scaled_half, "row", axis=0, tiled=True)
        blocks = gathered.reshape(-1, tile_side, half_width)
        summed = tile_products(
            tiles, tile_rows, tile_cols, identity_slot, 0, my_count, blocks, row_span
        )
        partial_value = summed.reshape(row_span * tile_side, half_width)
        new_half = inv_root * lax.psum_scatter(
            partial_value, "col", scatter_dimension=0, tiled=True
        )
        residual = join_halves(new_half)
        if previous is not None:
            residual = residual - full_dot(previous, betas[-1].T)
        alpha_block = lax.psum(full_dot(current.T, residual), ("row", "col"))
        residual = residual - full_dot(current, alpha_block)
        gram_matrix = lax.psum(full_dot(residual.T, residual), ("row", "col"))
        following, factor = factorize(gram_matrix, residual)
        alphas.append(alpha_block)
        betas.append(factor.T)
        previous, current = (current, following)
    final_half = lax.dynamic_slice_in_dim(current, side * half_width, half_width, 1)
    return (final_half, jnp.stack(alphas), jnp.stack(betas))


LAST = (((1,), (1,)), ((), ()))


def dot_last(left, right):
    return lax.dot_general(
        left, right, LAST, precision=lax.Precision.HIGHEST, preferred_element_type=jnp.float32
    )


def split_two(value):
    high = value.astype(jnp.bfloat16)
    low = (value - high.astype(jnp.float32)).astype(jnp.bfloat16)
    return high, low


def triangular_parts(gram):
    width = gram.shape[0]
    rows = lax.broadcasted_iota(jnp.int32, (width, width), 0)
    lanes = lax.broadcasted_iota(jnp.int32, (width, width), 1)
    upper = gram
    inverse = (rows == lanes).astype(jnp.float32)
    pivots = []
    group = 8
    for first in range(0, width, group):
        columns = [
            jnp.broadcast_to(upper[:, at : at + 1], (width, width))
            for at in range(first, first + group)
        ]
        for at in range(first, first + group):
            column = columns[at - first]
            pivot = column[at : at + 1, :]
            pivots.append(pivot)
            factor = jnp.where(rows > at, column * (1.0 / pivot), 0.0)
            for later in range(at + 1, first + group):
                other = columns[later - first]
                columns[later - first] = other - factor * other[at : at + 1, :]
            upper = upper - factor * upper[at : at + 1, :]
            inverse = inverse - factor * inverse[at : at + 1, :]
    scale = 1.0 / jnp.sqrt(jnp.concatenate(pivots, axis=0))
    return jnp.where(lanes >= rows, upper * scale, 0.0), inverse * scale


def lanczos_kernel(
    n_row, n_col, n_sub,
    rows_ref, cols_ref, count_ref, tiles_ref, start_ref,
    panel_ref, alphas_ref, betas_ref,
    tiles_buf, tile_high, tile_low, start_buf, sums_buf, part_buf,
    root_ref, current_ref, previous_ref, residual_ref,
    tile_sem, start_send, start_recv, sums_send, sums_recv, part_send, part_recv,
):
    slots, side, _ = tiles_ref.shape
    half = side // n_sub
    local_cols = slots // n_col
    width = part_buf.shape[2]
    half_width = width // n_sub
    devices = n_row * n_col * n_sub
    row = lax.axis_index("row")
    col = lax.axis_index("col")
    sub = lax.axis_index("sub")
    me = (row * n_col + col) * n_sub + sub

    def place(peer):
        return {
            "row": peer // (n_col * n_sub),
            "col": (peer // n_sub) % n_col,
            "sub": peer % n_sub,
        }

    def other(step):
        return lax.rem(me + step, devices)

    tile_copies = []
    for slot in range(slots):
        copy = pltpu.make_async_copy(
            tiles_ref.at[slot, pl.ds(pl.multiple_of(sub * half, half), half), :],
            tiles_buf.at[slot],
            tile_sem.at[slot],
        )
        copy.start()
        tile_copies.append(copy)

    barrier = pltpu.get_barrier_semaphore()
    for step in range(1, devices):
        pl.semaphore_signal(
            barrier, inc=1, device_id=place(other(step)), device_id_type=pl.DeviceIdType.MESH
        )
    start_buf[me] = start_ref[...].T
    pl.semaphore_wait(barrier, devices - 1)

    def copies(buf, send, recv):
        return [
            pltpu.make_async_remote_copy(
                src_ref=buf.at[me],
                dst_ref=buf.at[me],
                send_sem=send.at[step],
                recv_sem=recv.at[me],
                device_id=place(other(step)),
                device_id_type=pl.DeviceIdType.MESH,
            )
            for step in range(1, devices)
        ]

    def send_all(buf, send, recv):
        for copy in copies(buf, send, recv):
            copy.start()

    def wait_all(buf, send, recv):
        for step in range(1, devices):
            peer = other(step)
            pltpu.make_async_remote_copy(
                src_ref=buf.at[peer],
                dst_ref=buf.at[peer],
                send_sem=send.at[step],
                recv_sem=recv.at[peer],
                device_id=place(peer),
                device_id_type=pl.DeviceIdType.MESH,
            ).wait_recv()

    def wait_sent(buf, send, recv):
        for copy in copies(buf, send, recv):
            copy.wait_send()

    send_all(start_buf, start_send, start_recv)

    for copy in tile_copies:
        copy.wait()
    for block in range(n_col):
        for column in range(local_cols):
            slot = jnp.int32(0)
            for candidate in range(slots):
                here = (rows_ref[candidate] == block) & (cols_ref[candidate] == column)
                slot = jnp.where(here, candidate, slot)
            in_use = jnp.where(slot < count_ref[0], 1.0, 0.0)
            high, low = split_two(tiles_buf[slot] * in_use)
            at = (slice(block * half, (block + 1) * half), slice(column * side, (column + 1) * side))
            tile_high[at] = high
            tile_low[at] = low
    ones = jnp.ones((8, local_cols * side), jnp.bfloat16)
    sums_buf[me] = lax.dot_general(
        ones, tile_high[...], LAST, preferred_element_type=jnp.float32
    ) + lax.dot_general(ones, tile_low[...], LAST, preferred_element_type=jnp.float32)
    send_all(sums_buf, sums_send, sums_recv)

    wait_all(start_buf, start_send, start_recv)
    for block in range(n_row * n_col):
        for part in range(n_sub):
            residual_ref[
                part * half_width : (part + 1) * half_width, block * side : (block + 1) * side
            ] = start_buf[block * n_sub + part]

    def orthonormalize(at):
        panel = residual_ref[...]
        upper, inverse = triangular_parts(dot_last(panel, panel))
        betas_ref[at] = upper
        current_ref[...] = full_dot(inverse, panel)
        return upper

    beta = orthonormalize(0)

    def assemble(buf, target, finish):
        for r in range(n_row):
            for s in range(n_sub):
                total = buf[(r * n_col) * n_sub + s]
                for c in range(1, n_col):
                    total = total + buf[(r * n_col + c) * n_sub + s]
                for block in range(n_col):
                    first = (r * n_col + block) * side + s * half
                    target[:, first : first + half] = finish(
                        total[:, block * half : (block + 1) * half], first
                    )

    wait_all(sums_buf, sums_send, sums_recv)
    assemble(sums_buf, root_ref, lambda total, first: 1.0 / jnp.sqrt(1.0 + total))

    for iteration in range(alphas_ref.shape[0]):
        highs, lows = [], []
        for column in range(local_cols):
            at = pl.ds(pl.multiple_of((column * n_col + col) * side, side), side)
            high, low = split_two(current_ref[:, at] * root_ref[0:1, at])
            highs.append(high)
            lows.append(low)
        high = jnp.concatenate(highs, axis=1)
        both = jnp.concatenate([high, jnp.concatenate(lows, axis=1)], axis=0)
        first = lax.dot_general(both, tile_high[...], LAST, preferred_element_type=jnp.float32)
        second = lax.dot_general(high, tile_low[...], LAST, preferred_element_type=jnp.float32)
        buf = part_buf.at[iteration]
        send = part_send.at[iteration]
        recv = part_recv.at[iteration]
        buf[me] = first[:width] + (first[width:] + second)
        send_all(buf, send, recv)
        wait_all(buf, send, recv)
        assemble(
            buf, residual_ref, lambda total, first: total * root_ref[0:1, first : first + half]
        )
        residual = residual_ref[...]
        if iteration > 0:
            residual = residual - full_dot(beta, previous_ref[...])
        current = current_ref[...]
        alpha = dot_last(current, residual)
        alphas_ref[iteration] = alpha
        residual_ref[...] = residual - full_dot(alpha.T, current)
        previous_ref[...] = current
        beta = orthonormalize(iteration + 1)

    own = pl.ds(pl.multiple_of((row * n_col + col) * side, side), side)
    rows_own = pl.ds(pl.multiple_of(sub * half_width, half_width), half_width)
    panel_ref[...] = current_ref[rows_own, own].T

    wait_sent(start_buf, start_send, start_recv)
    wait_sent(sums_buf, sums_send, sums_recv)
    for iteration in range(alphas_ref.shape[0]):
        wait_sent(part_buf.at[iteration], part_send.at[iteration], part_recv.at[iteration])


def dense_on_device(tiles, tile_rows, tile_cols, tile_counts, start_panel):
    n_row, n_col, n_sub = (lax.axis_size(name) for name in ("row", "col", "sub"))
    slots, side, _ = tiles.shape
    half_width = start_panel.shape[1]
    width = half_width * n_sub
    half = side // n_sub
    devices = n_row * n_col * n_sub
    nodes = n_row * n_col * side
    in_vmem = pl.BlockSpec(memory_space=pltpu.VMEM)
    in_smem = pl.BlockSpec(memory_space=pltpu.SMEM)
    f32 = jnp.float32
    dma = pltpu.SemaphoreType.DMA
    return pl.pallas_call(
        functools.partial(lanczos_kernel, n_row, n_col, n_sub),
        out_shape=(
            jax.ShapeDtypeStruct(start_panel.shape, f32),
            jax.ShapeDtypeStruct((ITERS, width, width), f32),
            jax.ShapeDtypeStruct((ITERS + 1, width, width), f32),
        ),
        in_specs=[in_smem, in_smem, in_smem, pl.BlockSpec(memory_space=pl.ANY), in_vmem],
        out_specs=(in_vmem, in_vmem, in_vmem),
        scratch_shapes=[
            pltpu.VMEM((slots, half, side), f32),
            pltpu.VMEM((n_col * half, slots // n_col * side), jnp.bfloat16),
            pltpu.VMEM((n_col * half, slots // n_col * side), jnp.bfloat16),
            pltpu.VMEM((devices, half_width, side), f32),
            pltpu.VMEM((devices, 8, n_col * half), f32),
            pltpu.VMEM((ITERS, devices, width, n_col * half), f32),
            pltpu.VMEM((8, nodes), f32),
            pltpu.VMEM((width, nodes), f32),
            pltpu.VMEM((width, nodes), f32),
            pltpu.VMEM((width, nodes), f32),
            dma((slots,)),
            dma((devices,)),
            dma((devices,)),
            dma((devices,)),
            dma((devices,)),
            dma((ITERS, devices)),
            dma((ITERS, devices)),
        ],
        compiler_params=pltpu.CompilerParams(
            collective_id=0, has_side_effects=True, vmem_limit_bytes=40 * 2**20
        ),
    )(tile_rows, tile_cols, tile_counts, tiles, start_panel)


def on_one_device(tiles, tile_rows, tile_cols, tile_counts, start_panel):
    tile_side = tiles.shape[1]
    one_block = start_panel.shape[0] == tile_side
    covered = tiles.shape[0] == lax.axis_size("row") * lax.axis_size("col")
    form = dense_on_device if one_block and covered else on_device
    return form(tiles, tile_rows, tile_cols, tile_counts, start_panel)


def solution(mesh):
    return jax.shard_map(
        on_one_device,
        mesh=mesh,
        in_specs=(
            P(("parts", "row", "col"), None, None),
            P(("parts", "row", "col")),
            P(("parts", "row", "col")),
            P(("parts", "row", "col")),
            P(("parts", "row", "col"), "sub"),
        ),
        out_specs=(
            P(("parts", "row", "col"), "sub"),
            P("parts", None, None),
            P("parts", None, None),
        ),
        check_vma=False,
    )
```

```python
import functools

import jax
import jax.numpy as jnp
from jax import lax
from jax.experimental import pallas as pl
from jax.experimental.pallas import tpu as pltpu
from jax.sharding import PartitionSpec as P

ITERS = 3


def full_dot(left, right):
    return jnp.dot(left, right, precision=lax.Precision.HIGHEST)


def join_halves(half):
    return lax.all_gather(half, "sub", axis=1, tiled=True)


def factorize(gram_matrix, panel):
    factor = jnp.linalg.cholesky(gram_matrix)
    result = jax.scipy.linalg.solve_triangular(factor, panel.T, lower=True).T
    return (result, factor)


def tile_products(
    pooled_tiles, pooled_rows, pooled_cols, slot_of, first_index, end_index, blocks, row_total
):
    tile_side = pooled_tiles.shape[1]
    half_width = blocks.shape[2]
    per_turn = 4
    turn_count = (end_index - first_index + per_turn - 1) // per_turn

    def one_turn(position, summed):
        virtual = first_index + position * per_turn + jnp.arange(per_turn, dtype=jnp.int32)
        active = virtual < end_index
        clamped = jnp.clip(slot_of(virtual), 0, pooled_tiles.shape[0] - 1)
        chosen = jnp.take(pooled_tiles, clamped, axis=0)
        needed = jnp.take(blocks, jnp.take(pooled_cols, clamped), axis=0)
        product = jnp.einsum("gab,gbc->gac", chosen, needed, precision=lax.Precision.HIGHEST)
        targets = jnp.take(pooled_rows, clamped)
        select = (
            (targets[:, None] == jnp.arange(row_total, dtype=jnp.int32)[None, :]) & active[:, None]
        ).astype(jnp.float32)
        return summed + jnp.einsum("gr,gac->rac", select, product, precision=lax.Precision.HIGHEST)

    empty = jnp.zeros((row_total, tile_side, half_width), jnp.float32)
    return lax.fori_loop(0, turn_count, one_turn, empty)


def on_device(tiles, tile_rows, tile_cols, tile_counts, start_panel):
    slot_count = tiles.shape[0]
    tile_side = tiles.shape[1]
    local_rows = start_panel.shape[0]
    half_width = start_panel.shape[1]
    local_blocks = local_rows // tile_side
    row_span = local_blocks * lax.axis_size("col")
    my_count = tile_counts[0]
    side = lax.axis_index("sub")
    own_active = jnp.arange(slot_count, dtype=jnp.int32) < my_count
    in_use = own_active.astype(jnp.float32)
    row_sums = jnp.sum(tiles, axis=2)
    placing = (tile_rows[:, None] == jnp.arange(row_span, dtype=jnp.int32)[None, :]).astype(
        jnp.float32
    ) * in_use[:, None]
    partial_degree = full_dot(placing.T, row_sums).reshape(-1)
    degree = 1.0 + lax.psum_scatter(partial_degree, "col", scatter_dimension=0, tiled=True)
    inv_root = (1.0 / jnp.sqrt(degree))[:, None]

    def identity_slot(virtual):
        return virtual

    start_full = join_halves(start_panel)
    start_gram = lax.psum(full_dot(start_full.T, start_full), ("row", "col"))
    current, factor = factorize(start_gram, start_full)
    betas = [factor.T]
    alphas = []
    previous = None
    for iteration in range(ITERS):
        current_half = lax.dynamic_slice_in_dim(current, side * half_width, half_width, 1)
        scaled_half = inv_root * current_half
        gathered = lax.all_gather(scaled_half, "row", axis=0, tiled=True)
        blocks = gathered.reshape(-1, tile_side, half_width)
        summed = tile_products(
            tiles, tile_rows, tile_cols, identity_slot, 0, my_count, blocks, row_span
        )
        partial_value = summed.reshape(row_span * tile_side, half_width)
        new_half = inv_root * lax.psum_scatter(
            partial_value, "col", scatter_dimension=0, tiled=True
        )
        residual = join_halves(new_half)
        if previous is not None:
            residual = residual - full_dot(previous, betas[-1].T)
        alpha_block = lax.psum(full_dot(current.T, residual), ("row", "col"))
        residual = residual - full_dot(current, alpha_block)
        gram_matrix = lax.psum(full_dot(residual.T, residual), ("row", "col"))
        following, factor = factorize(gram_matrix, residual)
        alphas.append(alpha_block)
        betas.append(factor.T)
        previous, current = (current, following)
    final_half = lax.dynamic_slice_in_dim(current, side * half_width, half_width, 1)
    return (final_half, jnp.stack(alphas), jnp.stack(betas))


LAST = (((1,), (1,)), ((), ()))


def dot_last(left, right):
    return lax.dot_general(
        left, right, LAST, precision=lax.Precision.HIGHEST, preferred_element_type=jnp.float32
    )


def split_two(value):
    high = value.astype(jnp.bfloat16)
    low = (value - high.astype(jnp.float32)).astype(jnp.bfloat16)
    return high, low


def triangular_parts(gram):
    width = gram.shape[0]
    rows = lax.broadcasted_iota(jnp.int32, (width, width), 0)
    lanes = lax.broadcasted_iota(jnp.int32, (width, width), 1)
    upper = gram
    inverse = (rows == lanes).astype(jnp.float32)
    pivots = []
    group = 8
    for first in range(0, width, group):
        columns = [
            jnp.broadcast_to(upper[:, at : at + 1], (width, width))
            for at in range(first, first + group)
        ]
        for at in range(first, first + group):
            column = columns[at - first]
            pivot = column[at : at + 1, :]
            pivots.append(pivot)
            factor = jnp.where(rows > at, column * (1.0 / pivot), 0.0)
            for later in range(at + 1, first + group):
                other = columns[later - first]
                columns[later - first] = other - factor * other[at : at + 1, :]
            upper = upper - factor * upper[at : at + 1, :]
            inverse = inverse - factor * inverse[at : at + 1, :]
    scale = 1.0 / jnp.sqrt(jnp.concatenate(pivots, axis=0))
    return jnp.where(lanes >= rows, upper * scale, 0.0), inverse * scale


def lanczos_kernel(
    n_row, n_col, n_sub,
    rows_ref, cols_ref, count_ref, tiles_ref, start_ref,
    panel_ref, alphas_ref, betas_ref,
    tiles_buf, tile_high, tile_low, start_buf, sums_buf, mine_buf, theirs_buf, piece_buf,
    root_ref, current_ref, previous_ref, residual_ref,
    tile_sem, sums_send, sums_recv, start_send, start_recv, start_pass, start_took,
    half_send, half_recv, piece_send, piece_recv, piece_pass, piece_took,
):
    slots, side, _ = tiles_ref.shape
    half = side // n_sub
    local_cols = slots // n_col
    width = current_ref.shape[1]
    half_width = width // n_sub
    chips = n_row * n_col
    devices = chips * n_sub
    pieces = n_row * n_sub
    span = n_col * half
    row = lax.axis_index("row")
    col = lax.axis_index("col")
    sub = lax.axis_index("sub")
    chip = row * n_col + col
    me = chip * n_sub + sub

    def chip_place(peer):
        return {"row": peer // n_col, "col": lax.rem(peer, n_col), "sub": sub}

    def remote(buf, index, send, recv, place):
        return pltpu.make_async_remote_copy(
            src_ref=buf.at[index],
            dst_ref=buf.at[index],
            send_sem=send,
            recv_sem=recv,
            device_id=place,
            device_id_type=pl.DeviceIdType.MESH,
        )

    sent = []

    def push(copy):
        copy.start()
        sent.append(copy)

    tile_copies = []
    for slot in range(slots):
        copy = pltpu.make_async_copy(
            tiles_ref.at[slot, pl.ds(pl.multiple_of(sub * half, half), half), :],
            tiles_buf.at[slot],
            tile_sem.at[slot],
        )
        copy.start()
        tile_copies.append(copy)

    def device_place(peer):
        return {
            "row": peer // (n_col * n_sub),
            "col": lax.rem(peer // n_sub, n_col),
            "sub": lax.rem(peer, n_sub),
        }

    barrier = pltpu.get_barrier_semaphore()
    for step in range(1, devices):
        pl.semaphore_signal(
            barrier,
            inc=1,
            device_id=device_place(lax.rem(me + step, devices)),
            device_id_type=pl.DeviceIdType.MESH,
        )

    start_buf[chip * n_sub + sub] = start_ref[...].T
    for copy in tile_copies:
        copy.wait()
    for block in range(n_col):
        for column in range(local_cols):
            slot = jnp.int32(0)
            for candidate in range(slots):
                here = (rows_ref[candidate] == block) & (cols_ref[candidate] == column)
                slot = jnp.where(here, candidate, slot)
            in_use = jnp.where(slot < count_ref[0], 1.0, 0.0)
            high, low = split_two(tiles_buf[slot] * in_use)
            at = (slice(block * half, (block + 1) * half), slice(column * side, (column + 1) * side))
            tile_high[at] = high
            tile_low[at] = low
    ones = jnp.ones((8, local_cols * side), jnp.bfloat16)
    sums = lax.dot_general(
        ones, tile_high[...], LAST, preferred_element_type=jnp.float32
    ) + lax.dot_general(ones, tile_low[...], LAST, preferred_element_type=jnp.float32)
    sums_buf[me] = sums[0:1]
    pl.semaphore_wait(barrier, devices - 1)

    for step in range(1, chips):
        peer = lax.rem(chip + step, chips)
        push(remote(start_buf, me, start_send.at[step], start_recv.at[chip], chip_place(peer)))
    for step in range(1, n_sub):
        peer = lax.rem(sub + step, n_sub)
        push(remote(start_buf, me, start_pass.at[0, step], start_took.at[chip, sub], {"sub": peer}))
    for step in range(1, devices):
        peer = lax.rem(me + step, devices)
        push(remote(sums_buf, me, sums_send.at[step], sums_recv.at[me], device_place(peer)))
    for step in range(1, chips):
        peer = lax.rem(chip + step, chips)
        index = peer * n_sub + sub
        remote(
            start_buf, index, start_send.at[step], start_recv.at[peer], chip_place(peer)
        ).wait_recv()
        for hop in range(1, n_sub):
            to = lax.rem(sub + hop, n_sub)
            push(
                remote(
                    start_buf, index, start_pass.at[step, hop], start_took.at[peer, sub], {"sub": to}
                )
            )
    for step in range(1, devices):
        peer = lax.rem(me + step, devices)
        remote(
            sums_buf, peer, sums_send.at[step], sums_recv.at[peer], device_place(peer)
        ).wait_recv()
    for r in range(n_row):
        for s in range(n_sub):
            total = sums_buf[(r * n_col) * n_sub + s]
            for c in range(1, n_col):
                total = total + sums_buf[(r * n_col + c) * n_sub + s]
            root_ref[r * n_sub + s] = 1.0 / jnp.sqrt(1.0 + total)
    for hop in range(1, n_sub):
        source = lax.rem(sub + hop, n_sub)
        for step in range(chips):
            peer = lax.rem(chip + step, chips)
            remote(
                start_buf, peer * n_sub + source, start_pass.at[step, hop],
                start_took.at[peer, source], {"sub": source},
            ).wait_recv()
    for r in range(n_row):
        for c in range(n_col):
            for part in range(n_sub):
                for s in range(n_sub):
                    residual_ref[
                        r * n_sub + s,
                        part * half_width : (part + 1) * half_width,
                        c * half : (c + 1) * half,
                    ] = start_buf[(r * n_col + c) * n_sub + part, :, s * half : (s + 1) * half]

    def factorize_residual(at):
        gram = jnp.zeros((width, width), jnp.float32)
        for p in range(pieces):
            gram = gram + dot_last(residual_ref[p], residual_ref[p])
        upper, inverse = triangular_parts(gram)
        betas_ref[at] = upper
        return upper, inverse

    def orthonormalize(inverse):
        for p in range(pieces):
            current_ref[p] = full_dot(inverse, residual_ref[p])

    own_lanes = pl.ds(pl.multiple_of(col * half, half), half)
    own_piece = row * n_sub + sub
    root_own = root_ref[own_piece]
    for iteration in range(alphas_ref.shape[0]):
        highs, lows = [], []
        for p in range(pieces):
            high, low = split_two(residual_ref[p, :, own_lanes] * root_ref[p, :, own_lanes])
            highs.append(high)
            lows.append(low)
        high = jnp.concatenate(highs, axis=1)
        both = jnp.concatenate([high, jnp.concatenate(lows, axis=1)], axis=0)
        first = lax.dot_general(both, tile_high[...], LAST, preferred_element_type=jnp.float32)
        second = lax.dot_general(high, tile_low[...], LAST, preferred_element_type=jnp.float32)
        halves = theirs_buf.at[iteration]
        halves[col] = first[:width] + (first[width:] + second)
        for step in range(1, n_col):
            peer = lax.rem(col + step, n_col)
            push(
                remote(
                    halves, col, half_send.at[iteration, step], half_recv.at[iteration, col],
                    {"col": peer},
                )
            )
        upper, inverse = factorize_residual(iteration)
        for step in range(1, n_col):
            peer = lax.rem(col + step, n_col)
            remote(
                halves, peer, half_send.at[iteration, step], half_recv.at[iteration, peer],
                {"col": peer},
            ).wait_recv()
        total = halves[0]
        for c in range(1, n_col):
            total = total + halves[c]
        got = piece_buf.at[iteration]
        got[own_piece] = total * root_own
        for step in range(1, n_row):
            peer = lax.rem(row + step, n_row)
            push(
                remote(
                    got, own_piece, piece_send.at[iteration, step],
                    piece_recv.at[iteration, row], {"row": peer},
                )
            )
        for hop in range(1, n_sub):
            to = lax.rem(sub + hop, n_sub)
            push(
                remote(
                    got, own_piece, piece_pass.at[iteration, 0, hop],
                    piece_took.at[iteration, row, sub], {"sub": to},
                )
            )
        if iteration > 0:
            for p in range(pieces):
                previous_ref[p] = current_ref[p]
        orthonormalize(inverse)
        for step in range(1, n_row):
            peer = lax.rem(row + step, n_row)
            index = peer * n_sub + sub
            remote(
                got, index, piece_send.at[iteration, step], piece_recv.at[iteration, peer],
                {"row": peer},
            ).wait_recv()
            for hop in range(1, n_sub):
                to = lax.rem(sub + hop, n_sub)
                push(
                    remote(
                        got, index, piece_pass.at[iteration, step, hop],
                        piece_took.at[iteration, peer, sub], {"sub": to},
                    )
                )
        for hop in range(1, n_sub):
            source = lax.rem(sub + hop, n_sub)
            for step in range(n_row):
                peer = lax.rem(row + step, n_row)
                remote(
                    got, peer * n_sub + source, piece_pass.at[iteration, step, hop],
                    piece_took.at[iteration, peer, source], {"sub": source},
                ).wait_recv()
        alpha = jnp.zeros((width, width), jnp.float32)
        for p in range(pieces):
            if iteration > 0:
                mixed = full_dot(
                    jnp.concatenate([inverse, -upper], axis=1),
                    jnp.concatenate([got[p], previous_ref[p]], axis=0),
                )
            else:
                mixed = full_dot(inverse, got[p])
            residual_ref[p] = mixed
            alpha = alpha + dot_last(current_ref[p], mixed)
        alphas_ref[iteration] = alpha
        turned = alpha.T
        for p in range(pieces):
            residual_ref[p] = residual_ref[p] - full_dot(turned, current_ref[p])

    _, inverse = factorize_residual(alphas_ref.shape[0])
    rows_own = pl.ds(pl.multiple_of(sub * half_width, half_width), half_width)
    mine_buf[...] = inverse
    for s in range(n_sub):
        panel_ref[s * half : (s + 1) * half, :] = full_dot(
            mine_buf[rows_own, :], residual_ref[row * n_sub + s, :, own_lanes]
        ).T
    for copy in sent:
        copy.wait_send()


def dense_on_device(tiles, tile_rows, tile_cols, tile_counts, start_panel):
    n_row, n_col, n_sub = (lax.axis_size(name) for name in ("row", "col", "sub"))
    slots, side, _ = tiles.shape
    half_width = start_panel.shape[1]
    width = half_width * n_sub
    half = side // n_sub
    devices = n_row * n_col * n_sub
    chips = n_row * n_col
    pieces = n_row * n_sub
    span = n_col * half
    in_vmem = pl.BlockSpec(memory_space=pltpu.VMEM)
    in_smem = pl.BlockSpec(memory_space=pltpu.SMEM)
    f32 = jnp.float32
    dma = pltpu.SemaphoreType.DMA
    return pl.pallas_call(
        functools.partial(lanczos_kernel, n_row, n_col, n_sub),
        out_shape=(
            jax.ShapeDtypeStruct(start_panel.shape, f32),
            jax.ShapeDtypeStruct((ITERS, width, width), f32),
            jax.ShapeDtypeStruct((ITERS + 1, width, width), f32),
        ),
        in_specs=[in_smem, in_smem, in_smem, pl.BlockSpec(memory_space=pl.ANY), in_vmem],
        out_specs=(in_vmem, in_vmem, in_vmem),
        scratch_shapes=[
            pltpu.VMEM((slots, half, side), f32),
            pltpu.VMEM((span, slots // n_col * side), jnp.bfloat16),
            pltpu.VMEM((span, slots // n_col * side), jnp.bfloat16),
            pltpu.VMEM((devices, half_width, side), f32),
            pltpu.VMEM((devices, 1, span), f32),
            pltpu.VMEM((width, width), f32),
            pltpu.VMEM((ITERS, n_col, width, span), f32),
            pltpu.VMEM((ITERS, pieces, width, span), f32),
            pltpu.VMEM((pieces, 1, span), f32),
            pltpu.VMEM((pieces, width, span), f32),
            pltpu.VMEM((pieces, width, span), f32),
            pltpu.VMEM((pieces, width, span), f32),
            dma((slots,)),
            dma((devices,)),
            dma((devices,)),
            dma((chips,)),
            dma((chips,)),
            dma((chips, n_sub)),
            dma((chips, n_sub)),
            dma((ITERS, n_col)),
            dma((ITERS, n_col)),
            dma((ITERS, n_row)),
            dma((ITERS, n_row)),
            dma((ITERS, n_row, n_sub)),
            dma((ITERS, n_row, n_sub)),
        ],
        compiler_params=pltpu.CompilerParams(
            collective_id=0, has_side_effects=True, vmem_limit_bytes=40 * 2**20
        ),
    )(tile_rows, tile_cols, tile_counts, tiles, start_panel)


def on_one_device(tiles, tile_rows, tile_cols, tile_counts, start_panel):
    tile_side = tiles.shape[1]
    one_block = start_panel.shape[0] == tile_side
    covered = tiles.shape[0] == lax.axis_size("row") * lax.axis_size("col")
    form = dense_on_device if one_block and covered else on_device
    return form(tiles, tile_rows, tile_cols, tile_counts, start_panel)


def solution(mesh):
    return jax.shard_map(
        on_one_device,
        mesh=mesh,
        in_specs=(
            P(("parts", "row", "col"), None, None),
            P(("parts", "row", "col")),
            P(("parts", "row", "col")),
            P(("parts", "row", "col")),
            P(("parts", "row", "col"), "sub"),
        ),
        out_specs=(
            P(("parts", "row", "col"), "sub"),
            P("parts", None, None),
            P("parts", None, None),
        ),
        check_vma=False,
    )
```

```python
import functools

import jax
import jax.numpy as jnp
from jax import lax
from jax.experimental import pallas as pl
from jax.experimental.pallas import tpu as pltpu
from jax.sharding import PartitionSpec as P

ITERS = 3


def full_dot(left, right):
    return jnp.dot(left, right, precision=lax.Precision.HIGHEST)


def join_halves(half):
    return lax.all_gather(half, "sub", axis=1, tiled=True)


def factorize(gram_matrix, panel):
    factor = jnp.linalg.cholesky(gram_matrix)
    result = jax.scipy.linalg.solve_triangular(factor, panel.T, lower=True).T
    return (result, factor)


def tile_products(
    pooled_tiles, pooled_rows, pooled_cols, slot_of, first_index, end_index, blocks, row_total
):
    tile_side = pooled_tiles.shape[1]
    half_width = blocks.shape[2]
    per_turn = 4
    turn_count = (end_index - first_index + per_turn - 1) // per_turn

    def one_turn(position, summed):
        virtual = first_index + position * per_turn + jnp.arange(per_turn, dtype=jnp.int32)
        active = virtual < end_index
        clamped = jnp.clip(slot_of(virtual), 0, pooled_tiles.shape[0] - 1)
        chosen = jnp.take(pooled_tiles, clamped, axis=0)
        needed = jnp.take(blocks, jnp.take(pooled_cols, clamped), axis=0)
        product = jnp.einsum("gab,gbc->gac", chosen, needed, precision=lax.Precision.HIGHEST)
        targets = jnp.take(pooled_rows, clamped)
        select = (
            (targets[:, None] == jnp.arange(row_total, dtype=jnp.int32)[None, :]) & active[:, None]
        ).astype(jnp.float32)
        return summed + jnp.einsum("gr,gac->rac", select, product, precision=lax.Precision.HIGHEST)

    empty = jnp.zeros((row_total, tile_side, half_width), jnp.float32)
    return lax.fori_loop(0, turn_count, one_turn, empty)


def on_device(tiles, tile_rows, tile_cols, tile_counts, start_panel):
    slot_count = tiles.shape[0]
    tile_side = tiles.shape[1]
    local_rows = start_panel.shape[0]
    half_width = start_panel.shape[1]
    local_blocks = local_rows // tile_side
    row_span = local_blocks * lax.axis_size("col")
    my_count = tile_counts[0]
    side = lax.axis_index("sub")
    own_active = jnp.arange(slot_count, dtype=jnp.int32) < my_count
    in_use = own_active.astype(jnp.float32)
    row_sums = jnp.sum(tiles, axis=2)
    placing = (tile_rows[:, None] == jnp.arange(row_span, dtype=jnp.int32)[None, :]).astype(
        jnp.float32
    ) * in_use[:, None]
    partial_degree = full_dot(placing.T, row_sums).reshape(-1)
    degree = 1.0 + lax.psum_scatter(partial_degree, "col", scatter_dimension=0, tiled=True)
    inv_root = (1.0 / jnp.sqrt(degree))[:, None]

    def identity_slot(virtual):
        return virtual

    start_full = join_halves(start_panel)
    start_gram = lax.psum(full_dot(start_full.T, start_full), ("row", "col"))
    current, factor = factorize(start_gram, start_full)
    betas = [factor.T]
    alphas = []
    previous = None
    for iteration in range(ITERS):
        current_half = lax.dynamic_slice_in_dim(current, side * half_width, half_width, 1)
        scaled_half = inv_root * current_half
        gathered = lax.all_gather(scaled_half, "row", axis=0, tiled=True)
        blocks = gathered.reshape(-1, tile_side, half_width)
        summed = tile_products(
            tiles, tile_rows, tile_cols, identity_slot, 0, my_count, blocks, row_span
        )
        partial_value = summed.reshape(row_span * tile_side, half_width)
        new_half = inv_root * lax.psum_scatter(
            partial_value, "col", scatter_dimension=0, tiled=True
        )
        residual = join_halves(new_half)
        if previous is not None:
            residual = residual - full_dot(previous, betas[-1].T)
        alpha_block = lax.psum(full_dot(current.T, residual), ("row", "col"))
        residual = residual - full_dot(current, alpha_block)
        gram_matrix = lax.psum(full_dot(residual.T, residual), ("row", "col"))
        following, factor = factorize(gram_matrix, residual)
        alphas.append(alpha_block)
        betas.append(factor.T)
        previous, current = (current, following)
    final_half = lax.dynamic_slice_in_dim(current, side * half_width, half_width, 1)
    return (final_half, jnp.stack(alphas), jnp.stack(betas))


LAST = (((1,), (1,)), ((), ()))


def dot_last(left, right):
    return lax.dot_general(
        left, right, LAST, precision=lax.Precision.HIGHEST, preferred_element_type=jnp.float32
    )


def split_two(value):
    high = value.astype(jnp.bfloat16)
    low = (value - high.astype(jnp.float32)).astype(jnp.bfloat16)
    return high, low


def triangular_parts(gram):
    width = gram.shape[0]
    rows = lax.broadcasted_iota(jnp.int32, (width, width), 0)
    lanes = lax.broadcasted_iota(jnp.int32, (width, width), 1)
    upper = gram
    inverse = (rows == lanes).astype(jnp.float32)
    pivots = []
    group = 8
    for first in range(0, width, group):
        columns = [
            jnp.broadcast_to(upper[:, at : at + 1], (width, width))
            for at in range(first, first + group)
        ]
        for at in range(first, first + group):
            column = columns[at - first]
            pivot = column[at : at + 1, :]
            pivots.append(pivot)
            factor = jnp.where(rows > at, column * (1.0 / pivot), 0.0)
            for later in range(at + 1, first + group):
                other = columns[later - first]
                columns[later - first] = other - factor * other[at : at + 1, :]
            upper = upper - factor * upper[at : at + 1, :]
            inverse = inverse - factor * inverse[at : at + 1, :]
    scale = 1.0 / jnp.sqrt(jnp.concatenate(pivots, axis=0))
    return jnp.where(lanes >= rows, upper * scale, 0.0), inverse * scale


def lanczos_kernel(
    n_row, n_col, n_sub,
    rows_any, cols_any, count_any, tiles_ref, start_ref,
    panel_ref, alphas_ref, betas_ref,
    rows_ref, cols_ref, count_ref, small_sem, tiles_buf, tile_high, tile_low, start_buf, sums_buf, mine_buf, theirs_buf, piece_buf,
    root_ref, current_ref, previous_ref, residual_ref,
    tile_sem, sums_send, sums_recv, root_send, root_recv, root_pass, root_took,
    start_x_send, start_x_recv, start_send, start_recv, start_pass, start_took,
    half_send, half_recv, piece_send, piece_recv, piece_pass, piece_took,
):
    slots, side, _ = tiles_ref.shape
    half = side // n_sub
    local_cols = slots // n_col
    width = current_ref.shape[1]
    half_width = width // n_sub
    chips = n_row * n_col
    pieces = n_row * n_sub
    span = n_col * half
    row = lax.axis_index("row")
    col = lax.axis_index("col")
    sub = lax.axis_index("sub")
    chip = row * n_col + col

    def remote(buf, index, send, recv, place):
        return pltpu.make_async_remote_copy(
            src_ref=buf.at[index],
            dst_ref=buf.at[index],
            send_sem=send,
            recv_sem=recv,
            device_id=place,
            device_id_type=pl.DeviceIdType.MESH,
        )

    sent = []

    def push(copy):
        copy.start()
        sent.append(copy)

    small_copies = [
        pltpu.make_async_copy(source, target, small_sem.at[at])
        for at, (source, target) in enumerate(
            (
                (rows_any, rows_ref),
                (cols_any, cols_ref),
                (count_any, count_ref),
                (start_ref, start_buf.at[chip, sub]),
            )
        )
    ]
    for copy in small_copies:
        copy.start()
    tile_copies = []
    for slot in range(slots):
        copy = pltpu.make_async_copy(
            tiles_ref.at[slot, pl.ds(pl.multiple_of(sub * half, half), half), :],
            tiles_buf.at[slot],
            tile_sem.at[slot],
        )
        copy.start()
        tile_copies.append(copy)

    rows_apart = [lax.rem(row + step, n_row) for step in range(1, n_row)]
    cols_apart = [lax.rem(col + step, n_col) for step in range(1, n_col)]
    subs_apart = [lax.rem(sub + step, n_sub) for step in range(1, n_sub)]
    partners = (
        [{"row": peer} for peer in rows_apart]
        + [{"col": peer} for peer in cols_apart]
        + [{"sub": peer} for peer in subs_apart]
    )
    barrier = pltpu.get_barrier_semaphore()
    for partner in partners:
        pl.semaphore_signal(
            barrier, inc=1, device_id=partner, device_id_type=pl.DeviceIdType.MESH
        )

    for copy in small_copies + tile_copies:
        copy.wait()
    for block in range(n_col):
        for column in range(local_cols):
            slot = jnp.int32(0)
            for candidate in range(slots):
                here = (rows_ref[candidate] == block) & (cols_ref[candidate] == column)
                slot = jnp.where(here, candidate, slot)
            in_use = jnp.where(slot < count_ref[0], 1.0, 0.0)
            high, low = split_two(tiles_buf[slot] * in_use)
            at = (slice(block * half, (block + 1) * half), slice(column * side, (column + 1) * side))
            tile_high[at] = high
            tile_low[at] = low
    ones = jnp.ones((8, local_cols * side), jnp.bfloat16)
    sums = lax.dot_general(
        ones, tile_high[...], LAST, preferred_element_type=jnp.float32
    ) + lax.dot_general(ones, tile_low[...], LAST, preferred_element_type=jnp.float32)
    sums_buf[col] = sums[0:1]
    pl.semaphore_wait(barrier, len(partners))

    def start_from(source_row, source_col, source_sub):
        return start_buf.at[source_row * n_col + source_col, source_sub]

    def move(ref, send, recv, place):
        return pltpu.make_async_remote_copy(
            src_ref=ref,
            dst_ref=ref,
            send_sem=send,
            recv_sem=recv,
            device_id=place,
            device_id_type=pl.DeviceIdType.MESH,
        )

    def start_along_cols(step, source_col):
        return move(
            start_from(row, source_col, sub), start_x_send.at[step], start_x_recv.at[source_col],
            {"col": cols_apart[step]},
        )

    def start_along_rows(step, source_row, source_col):
        return move(
            start_from(source_row, source_col, sub),
            start_send.at[step, source_col],
            start_recv.at[source_row, source_col],
            {"row": rows_apart[step]},
        )

    def start_along_subs(step, source_row, source_col, source_sub):
        return move(
            start_from(source_row, source_col, source_sub),
            start_pass.at[step, source_row, source_col],
            start_took.at[source_row, source_col, source_sub],
            {"sub": subs_apart[step]},
        )

    for step in range(n_col - 1):
        push(
            move(
                sums_buf.at[col], sums_send.at[step], sums_recv.at[col], {"col": cols_apart[step]}
            )
        )
        push(start_along_cols(step, col))
    for step in range(n_row - 1):
        push(start_along_rows(step, row, col))
    for step in range(n_sub - 1):
        push(start_along_subs(step, row, col, sub))

    for step in range(n_col - 1):
        peer = cols_apart[step]
        move(
            sums_buf.at[peer], sums_send.at[step], sums_recv.at[peer], {"col": peer}
        ).wait_recv()
    total = sums_buf[0]
    for c in range(1, n_col):
        total = total + sums_buf[c]
    root_own = 1.0 / jnp.sqrt(1.0 + total)
    own_piece = row * n_sub + sub

    def root_along_rows(step, source_row):
        return move(
            root_ref.at[source_row * n_sub + sub], root_send.at[step], root_recv.at[source_row],
            {"row": rows_apart[step]},
        )

    def root_along_subs(step, source_row, source_sub):
        return move(
            root_ref.at[source_row * n_sub + source_sub],
            root_pass.at[step, source_row],
            root_took.at[source_row, source_sub],
            {"sub": subs_apart[step]},
        )

    root_ref[own_piece] = root_own
    for step in range(n_row - 1):
        push(root_along_rows(step, row))
    for step in range(n_sub - 1):
        push(root_along_subs(step, row, sub))
    for step in range(n_col - 1):
        peer = cols_apart[step]
        start_along_cols(step, peer).wait_recv()
        for hop in range(n_row - 1):
            push(start_along_rows(hop, row, peer))
        for hop in range(n_sub - 1):
            push(start_along_subs(hop, row, peer, sub))
    for step in range(n_row - 1):
        peer = rows_apart[step]
        root_along_rows(step, peer).wait_recv()
        for hop in range(n_sub - 1):
            push(root_along_subs(hop, peer, sub))
        start_along_rows(step, peer, col).wait_recv()
        for hop in range(n_sub - 1):
            push(start_along_subs(hop, peer, col, sub))
    for step in range(n_row - 1):
        peer = rows_apart[step]
        for source_col in cols_apart:
            start_along_rows(step, peer, source_col).wait_recv()
            for hop in range(n_sub - 1):
                push(start_along_subs(hop, peer, source_col, sub))
    for step in range(n_sub - 1):
        source = subs_apart[step]
        for peer in [row] + rows_apart:
            root_along_subs(step, peer, source).wait_recv()
            for source_col in [col] + cols_apart:
                start_along_subs(step, peer, source_col, source).wait_recv()
    for r in range(n_row):
        for c in range(n_col):
            for part in range(n_sub):
                for s in range(n_sub):
                    residual_ref[
                        r * n_sub + s,
                        part * half_width : (part + 1) * half_width,
                        c * half : (c + 1) * half,
                    ] = start_buf[r * n_col + c, part, :, s * half : (s + 1) * half]

    def factorize_residual(at):
        gram = jnp.zeros((width, width), jnp.float32)
        for p in range(pieces):
            gram = gram + dot_last(residual_ref[p], residual_ref[p])
        upper, inverse = triangular_parts(gram)
        betas_ref[at] = upper
        return upper, inverse

    def orthonormalize(inverse):
        for p in range(pieces):
            current_ref[p] = full_dot(inverse, residual_ref[p])

    own_lanes = pl.ds(pl.multiple_of(col * half, half), half)
    for iteration in range(alphas_ref.shape[0]):
        highs, lows = [], []
        for p in range(pieces):
            high, low = split_two(residual_ref[p, :, own_lanes] * root_ref[p, :, own_lanes])
            highs.append(high)
            lows.append(low)
        high = jnp.concatenate(highs, axis=1)
        both = jnp.concatenate([high, jnp.concatenate(lows, axis=1)], axis=0)
        first = lax.dot_general(both, tile_high[...], LAST, preferred_element_type=jnp.float32)
        second = lax.dot_general(high, tile_low[...], LAST, preferred_element_type=jnp.float32)
        halves = theirs_buf.at[iteration]
        halves[col] = first[:width] + (first[width:] + second)
        for step in range(1, n_col):
            peer = lax.rem(col + step, n_col)
            push(
                remote(
                    halves, col, half_send.at[iteration, step], half_recv.at[iteration, col],
                    {"col": peer},
                )
            )
        upper, inverse = factorize_residual(iteration)
        for step in range(1, n_col):
            peer = lax.rem(col + step, n_col)
            remote(
                halves, peer, half_send.at[iteration, step], half_recv.at[iteration, peer],
                {"col": peer},
            ).wait_recv()
        total = halves[0]
        for c in range(1, n_col):
            total = total + halves[c]
        got = piece_buf.at[iteration]
        got[own_piece] = total * root_own
        for step in range(1, n_row):
            peer = lax.rem(row + step, n_row)
            push(
                remote(
                    got, own_piece, piece_send.at[iteration, step],
                    piece_recv.at[iteration, row], {"row": peer},
                )
            )
        for hop in range(1, n_sub):
            to = lax.rem(sub + hop, n_sub)
            push(
                remote(
                    got, own_piece, piece_pass.at[iteration, 0, hop],
                    piece_took.at[iteration, row, sub], {"sub": to},
                )
            )
        if iteration > 0:
            for p in range(pieces):
                previous_ref[p] = current_ref[p]
        orthonormalize(inverse)
        for step in range(1, n_row):
            peer = lax.rem(row + step, n_row)
            index = peer * n_sub + sub
            remote(
                got, index, piece_send.at[iteration, step], piece_recv.at[iteration, peer],
                {"row": peer},
            ).wait_recv()
            for hop in range(1, n_sub):
                to = lax.rem(sub + hop, n_sub)
                push(
                    remote(
                        got, index, piece_pass.at[iteration, step, hop],
                        piece_took.at[iteration, peer, sub], {"sub": to},
                    )
                )
        for hop in range(1, n_sub):
            source = lax.rem(sub + hop, n_sub)
            for step in range(n_row):
                peer = lax.rem(row + step, n_row)
                remote(
                    got, peer * n_sub + source, piece_pass.at[iteration, step, hop],
                    piece_took.at[iteration, peer, source], {"sub": source},
                ).wait_recv()
        alpha = jnp.zeros((width, width), jnp.float32)
        for p in range(pieces):
            if iteration > 0:
                mixed = full_dot(
                    jnp.concatenate([inverse, -upper], axis=1),
                    jnp.concatenate([got[p], previous_ref[p]], axis=0),
                )
            else:
                mixed = full_dot(inverse, got[p])
            residual_ref[p] = mixed
            alpha = alpha + dot_last(current_ref[p], mixed)
        alphas_ref[iteration] = alpha
        turned = alpha.T
        for p in range(pieces):
            residual_ref[p] = residual_ref[p] - full_dot(turned, current_ref[p])

    _, inverse = factorize_residual(alphas_ref.shape[0])
    rows_own = pl.ds(pl.multiple_of(sub * half_width, half_width), half_width)
    mine_buf[...] = inverse
    for s in range(n_sub):
        panel_ref[:, s * half : (s + 1) * half] = full_dot(
            mine_buf[rows_own, :], residual_ref[row * n_sub + s, :, own_lanes]
        )
    for copy in sent:
        copy.wait_send()


def hand_out_kernel(*refs):
    count = len(refs) // 3
    sources, targets, held = refs[:count], refs[count : 2 * count], refs[2 * count : 3 * count]
    sem = refs[-1]
    inward = [
        pltpu.make_async_copy(source, here, sem.at[0, at])
        for at, (source, here) in enumerate(zip(sources, held))
    ]
    outward = [
        pltpu.make_async_copy(here, target, sem.at[1, at])
        for at, (here, target) in enumerate(zip(held, targets))
    ]
    for copy in inward:
        copy.start()
    for copy, onward in zip(inward, outward):
        copy.wait()
        onward.start()
    for copy in outward:
        copy.wait()


def hand_out(*arrays):
    in_hbm = pl.BlockSpec(memory_space=pltpu.HBM)
    return pl.pallas_call(
        hand_out_kernel,
        out_shape=tuple(jax.ShapeDtypeStruct(array.shape, array.dtype) for array in arrays),
        in_specs=[in_hbm] * len(arrays),
        out_specs=(in_hbm,) * len(arrays),
        scratch_shapes=[pltpu.VMEM(array.shape, array.dtype) for array in arrays]
        + [pltpu.SemaphoreType.DMA((2, len(arrays)))],
        compiler_params=pltpu.CompilerParams(vmem_limit_bytes=60 * 2**20),
    )(*arrays)


def dense_on_device(tiles, tile_rows, tile_cols, tile_counts, start_panel):
    n_row, n_col, n_sub = (lax.axis_size(name) for name in ("row", "col", "sub"))
    slots, side, _ = tiles.shape
    half_width = start_panel.shape[1]
    width = half_width * n_sub
    half = side // n_sub
    chips = n_row * n_col
    pieces = n_row * n_sub
    span = n_col * half
    in_vmem = pl.BlockSpec(memory_space=pltpu.VMEM)
    f32 = jnp.float32
    dma = pltpu.SemaphoreType.DMA
    panel, alphas, betas = pl.pallas_call(
        functools.partial(lanczos_kernel, n_row, n_col, n_sub),
        out_shape=(
            jax.ShapeDtypeStruct((half_width, side), f32),
            jax.ShapeDtypeStruct((ITERS, width, width), f32),
            jax.ShapeDtypeStruct((ITERS + 1, width, width), f32),
        ),
        in_specs=[pl.BlockSpec(memory_space=pltpu.HBM)] * 5,
        out_specs=(in_vmem, in_vmem, in_vmem),
        scratch_shapes=[
            pltpu.SMEM(tile_rows.shape, jnp.int32),
            pltpu.SMEM(tile_cols.shape, jnp.int32),
            pltpu.SMEM(tile_counts.shape, jnp.int32),
            dma((4,)),
            pltpu.VMEM((slots, half, side), f32),
            pltpu.VMEM((span, slots // n_col * side), jnp.bfloat16),
            pltpu.VMEM((span, slots // n_col * side), jnp.bfloat16),
            pltpu.VMEM((chips, n_sub, half_width, side), f32),
            pltpu.VMEM((n_col, 1, span), f32),
            pltpu.VMEM((width, width), f32),
            pltpu.VMEM((ITERS, n_col, width, span), f32),
            pltpu.VMEM((ITERS, pieces, width, span), f32),
            pltpu.VMEM((pieces, 1, span), f32),
            pltpu.VMEM((pieces, width, span), f32),
            pltpu.VMEM((pieces, width, span), f32),
            pltpu.VMEM((pieces, width, span), f32),
            dma((slots,)),
            dma((n_col,)),
            dma((n_col,)),
            dma((n_row,)),
            dma((n_row,)),
            dma((n_sub, n_row)),
            dma((n_row, n_sub)),
            dma((n_col,)),
            dma((n_col,)),
            dma((n_row, n_col)),
            dma((n_row, n_col)),
            dma((n_sub, n_row, n_col)),
            dma((n_row, n_col, n_sub)),
            dma((ITERS, n_col)),
            dma((ITERS, n_col)),
            dma((ITERS, n_row)),
            dma((ITERS, n_row)),
            dma((ITERS, n_row, n_sub)),
            dma((ITERS, n_row, n_sub)),
        ],
        compiler_params=pltpu.CompilerParams(
            collective_id=0, has_side_effects=True, vmem_limit_bytes=60 * 2**20
        ),
    )(tile_rows, tile_cols, tile_counts, tiles, start_panel.T)
    panel, alphas, betas = hand_out(panel, alphas, betas)
    return panel.T, alphas, betas


def on_one_device(tiles, tile_rows, tile_cols, tile_counts, start_panel):
    tile_side = tiles.shape[1]
    one_block = start_panel.shape[0] == tile_side
    covered = tiles.shape[0] == lax.axis_size("row") * lax.axis_size("col")
    form = dense_on_device if one_block and covered else on_device
    return form(tiles, tile_rows, tile_cols, tile_counts, start_panel)


def solution(mesh):
    return jax.shard_map(
        on_one_device,
        mesh=mesh,
        in_specs=(
            P(("parts", "row", "col"), None, None),
            P(("parts", "row", "col")),
            P(("parts", "row", "col")),
            P(("parts", "row", "col")),
            P(("parts", "row", "col"), "sub"),
        ),
        out_specs=(
            P(("parts", "row", "col"), "sub"),
            P("parts", None, None),
            P("parts", None, None),
        ),
        check_vma=False,
    )
```

```python
import functools

import jax
import jax.numpy as jnp
from jax import lax
from jax.experimental import pallas as pl
from jax.experimental.pallas import tpu as pltpu
from jax.sharding import PartitionSpec as P

ITERS = 3


def full_dot(left, right):
    return jnp.dot(left, right, precision=lax.Precision.HIGHEST)


def join_halves(half):
    return lax.all_gather(half, "sub", axis=1, tiled=True)


def factorize(gram_matrix, panel):
    factor = jnp.linalg.cholesky(gram_matrix)
    result = jax.scipy.linalg.solve_triangular(factor, panel.T, lower=True).T
    return (result, factor)


def tile_products(
    pooled_tiles, pooled_rows, pooled_cols, slot_of, first_index, end_index, blocks, row_total
):
    tile_side = pooled_tiles.shape[1]
    half_width = blocks.shape[2]
    per_turn = 4
    turn_count = (end_index - first_index + per_turn - 1) // per_turn

    def one_turn(position, summed):
        virtual = first_index + position * per_turn + jnp.arange(per_turn, dtype=jnp.int32)
        active = virtual < end_index
        clamped = jnp.clip(slot_of(virtual), 0, pooled_tiles.shape[0] - 1)
        chosen = jnp.take(pooled_tiles, clamped, axis=0)
        needed = jnp.take(blocks, jnp.take(pooled_cols, clamped), axis=0)
        product = jnp.einsum("gab,gbc->gac", chosen, needed, precision=lax.Precision.HIGHEST)
        targets = jnp.take(pooled_rows, clamped)
        select = (
            (targets[:, None] == jnp.arange(row_total, dtype=jnp.int32)[None, :]) & active[:, None]
        ).astype(jnp.float32)
        return summed + jnp.einsum("gr,gac->rac", select, product, precision=lax.Precision.HIGHEST)

    empty = jnp.zeros((row_total, tile_side, half_width), jnp.float32)
    return lax.fori_loop(0, turn_count, one_turn, empty)


def on_device(tiles, tile_rows, tile_cols, tile_counts, start_panel):
    slot_count = tiles.shape[0]
    tile_side = tiles.shape[1]
    local_rows = start_panel.shape[0]
    half_width = start_panel.shape[1]
    local_blocks = local_rows // tile_side
    row_span = local_blocks * lax.axis_size("col")
    my_count = tile_counts[0]
    side = lax.axis_index("sub")
    own_active = jnp.arange(slot_count, dtype=jnp.int32) < my_count
    in_use = own_active.astype(jnp.float32)
    row_sums = jnp.sum(tiles, axis=2)
    placing = (tile_rows[:, None] == jnp.arange(row_span, dtype=jnp.int32)[None, :]).astype(
        jnp.float32
    ) * in_use[:, None]
    partial_degree = full_dot(placing.T, row_sums).reshape(-1)
    degree = 1.0 + lax.psum_scatter(partial_degree, "col", scatter_dimension=0, tiled=True)
    inv_root = (1.0 / jnp.sqrt(degree))[:, None]

    def identity_slot(virtual):
        return virtual

    start_full = join_halves(start_panel)
    start_gram = lax.psum(full_dot(start_full.T, start_full), ("row", "col"))
    current, factor = factorize(start_gram, start_full)
    betas = [factor.T]
    alphas = []
    previous = None
    for iteration in range(ITERS):
        current_half = lax.dynamic_slice_in_dim(current, side * half_width, half_width, 1)
        scaled_half = inv_root * current_half
        gathered = lax.all_gather(scaled_half, "row", axis=0, tiled=True)
        blocks = gathered.reshape(-1, tile_side, half_width)
        summed = tile_products(
            tiles, tile_rows, tile_cols, identity_slot, 0, my_count, blocks, row_span
        )
        partial_value = summed.reshape(row_span * tile_side, half_width)
        new_half = inv_root * lax.psum_scatter(
            partial_value, "col", scatter_dimension=0, tiled=True
        )
        residual = join_halves(new_half)
        if previous is not None:
            residual = residual - full_dot(previous, betas[-1].T)
        alpha_block = lax.psum(full_dot(current.T, residual), ("row", "col"))
        residual = residual - full_dot(current, alpha_block)
        gram_matrix = lax.psum(full_dot(residual.T, residual), ("row", "col"))
        following, factor = factorize(gram_matrix, residual)
        alphas.append(alpha_block)
        betas.append(factor.T)
        previous, current = (current, following)
    final_half = lax.dynamic_slice_in_dim(current, side * half_width, half_width, 1)
    return (final_half, jnp.stack(alphas), jnp.stack(betas))


LAST = (((1,), (1,)), ((), ()))
PLAIN = (((1,), (0,)), ((), ()))


def dot_parts(left, right, dims):
    left_high, left_low = split_two(left)
    right_high, right_low = split_two(right)
    dot = functools.partial(
        lax.dot_general, dimension_numbers=dims, preferred_element_type=jnp.float32
    )
    both = dot(jnp.concatenate([left_high, left_low], axis=0), right_high)
    rows = left.shape[0]
    return both[:rows] + (both[rows:] + dot(left_high, right_low))


def dot_last(left, right):
    return dot_parts(left, right, LAST)


def split_two(value):
    high = value.astype(jnp.bfloat16)
    low = (value - high.astype(jnp.float32)).astype(jnp.bfloat16)
    return high, low


def triangular_parts(gram):
    width = gram.shape[0]
    rows = lax.broadcasted_iota(jnp.int32, (width, width), 0)
    lanes = lax.broadcasted_iota(jnp.int32, (width, width), 1)
    upper = gram
    inverse = (rows == lanes).astype(jnp.float32)
    pivots = []
    group = 8
    for first in range(0, width, group):
        columns = [
            jnp.broadcast_to(upper[:, at : at + 1], (width, width))
            for at in range(first, first + group)
        ]
        for at in range(first, first + group):
            column = columns[at - first]
            pivot = column[at : at + 1, :]
            pivots.append(pivot)
            factor = jnp.where(rows > at, column * (1.0 / pivot), 0.0)
            for later in range(at + 1, first + group):
                other = columns[later - first]
                columns[later - first] = other - factor * other[at : at + 1, :]
            upper = upper - factor * upper[at : at + 1, :]
            inverse = inverse - factor * inverse[at : at + 1, :]
    scale = 1.0 / jnp.sqrt(jnp.concatenate(pivots, axis=0))
    return jnp.where(lanes >= rows, upper * scale, 0.0), inverse * scale


def plain_dot(left, right):
    return dot_parts(left, right, PLAIN)


def lanczos_kernel(
    n_row, n_col, n_sub,
    rows_any, cols_any, count_any, tiles_ref, start_ref,
    panel_ref, alphas_ref, betas_ref,
    rows_ref, cols_ref, count_ref, small_sem, tiles_buf, tile_high, tile_low, start_buf, sums_buf, mine_buf, theirs_buf, piece_buf,
    root_ref, current_ref, previous_ref, residual_ref,
    tile_sem, sums_send, sums_recv, start_send, start_recv, start_pass, start_took,
    half_send, half_recv, piece_send, piece_recv, piece_pass, piece_took,
):
    slots, side, _ = tiles_ref.shape
    half = side // n_sub
    local_cols = slots // n_col
    width = current_ref.shape[1]
    half_width = width // n_sub
    chips = n_row * n_col
    devices = chips * n_sub
    pieces = n_row * n_sub
    span = n_col * half
    row = lax.axis_index("row")
    col = lax.axis_index("col")
    sub = lax.axis_index("sub")
    chip = row * n_col + col
    me = chip * n_sub + sub

    def chip_place(peer):
        return {"row": peer // n_col, "col": lax.rem(peer, n_col), "sub": sub}

    def remote(buf, index, send, recv, place):
        return pltpu.make_async_remote_copy(
            src_ref=buf.at[index],
            dst_ref=buf.at[index],
            send_sem=send,
            recv_sem=recv,
            device_id=place,
            device_id_type=pl.DeviceIdType.MESH,
        )

    sent = []

    def push(copy):
        copy.start()
        sent.append(copy)

    small_copies = [
        pltpu.make_async_copy(source, target, small_sem.at[at])
        for at, (source, target) in enumerate(
            (
                (rows_any, rows_ref),
                (cols_any, cols_ref),
                (count_any, count_ref),
                (start_ref, start_buf.at[me]),
            )
        )
    ]
    for copy in small_copies:
        copy.start()
    tile_copies = []
    for slot in range(slots):
        copy = pltpu.make_async_copy(
            tiles_ref.at[slot, pl.ds(pl.multiple_of(sub * half, half), half), :],
            tiles_buf.at[slot],
            tile_sem.at[slot],
        )
        copy.start()
        tile_copies.append(copy)

    def device_place(peer):
        return {
            "row": peer // (n_col * n_sub),
            "col": lax.rem(peer // n_sub, n_col),
            "sub": lax.rem(peer, n_sub),
        }

    barrier = pltpu.get_barrier_semaphore()
    for step in range(1, devices):
        pl.semaphore_signal(
            barrier,
            inc=1,
            device_id=device_place(lax.rem(me + step, devices)),
            device_id_type=pl.DeviceIdType.MESH,
        )

    for copy in small_copies + tile_copies:
        copy.wait()
    for block in range(n_col):
        for column in range(local_cols):
            slot = jnp.int32(0)
            for candidate in range(slots):
                here = (rows_ref[candidate] == block) & (cols_ref[candidate] == column)
                slot = jnp.where(here, candidate, slot)
            in_use = jnp.where(slot < count_ref[0], 1.0, 0.0)
            high, low = split_two(tiles_buf[slot] * in_use)
            at = (slice(block * half, (block + 1) * half), slice(column * side, (column + 1) * side))
            tile_high[at] = high
            tile_low[at] = low
    ones = jnp.ones((8, local_cols * side), jnp.bfloat16)
    sums = lax.dot_general(
        ones, tile_high[...], LAST, preferred_element_type=jnp.float32
    ) + lax.dot_general(ones, tile_low[...], LAST, preferred_element_type=jnp.float32)
    sums_buf[me] = sums[0:1]
    pl.semaphore_wait(barrier, devices - 1)

    for step in range(1, chips):
        peer = lax.rem(chip + step, chips)
        push(remote(start_buf, me, start_send.at[step], start_recv.at[chip], chip_place(peer)))
    for step in range(1, n_sub):
        peer = lax.rem(sub + step, n_sub)
        push(remote(start_buf, me, start_pass.at[0, step], start_took.at[chip, sub], {"sub": peer}))
    for step in range(1, devices):
        peer = lax.rem(me + step, devices)
        push(remote(sums_buf, me, sums_send.at[step], sums_recv.at[me], device_place(peer)))
    for step in range(chips - 1, 0, -1):
        peer = lax.rem(chip + step, chips)
        index = peer * n_sub + sub
        remote(
            start_buf, index, start_send.at[step], start_recv.at[peer], chip_place(peer)
        ).wait_recv()
        for hop in range(1, n_sub):
            to = lax.rem(sub + hop, n_sub)
            push(
                remote(
                    start_buf, index, start_pass.at[step, hop], start_took.at[peer, sub], {"sub": to}
                )
            )
    for step in range(1, devices):
        peer = lax.rem(me + step, devices)
        remote(
            sums_buf, peer, sums_send.at[step], sums_recv.at[peer], device_place(peer)
        ).wait_recv()
    for r in range(n_row):
        for s in range(n_sub):
            total = sums_buf[(r * n_col) * n_sub + s]
            for c in range(1, n_col):
                total = total + sums_buf[(r * n_col + c) * n_sub + s]
            root_ref[r * n_sub + s] = 1.0 / jnp.sqrt(1.0 + total)
    for hop in range(1, n_sub):
        source = lax.rem(sub + hop, n_sub)
        for step in range(chips):
            peer = lax.rem(chip + step, chips)
            remote(
                start_buf, peer * n_sub + source, start_pass.at[step, hop],
                start_took.at[peer, source], {"sub": source},
            ).wait_recv()
    for r in range(n_row):
        for c in range(n_col):
            for part in range(n_sub):
                for s in range(n_sub):
                    residual_ref[
                        r * n_sub + s,
                        part * half_width : (part + 1) * half_width,
                        c * half : (c + 1) * half,
                    ] = start_buf[(r * n_col + c) * n_sub + part, :, s * half : (s + 1) * half]

    def factorize_residual(at):
        gram = jnp.zeros((width, width), jnp.float32)
        for p in range(pieces):
            gram = gram + dot_last(residual_ref[p], residual_ref[p])
        upper, inverse = triangular_parts(gram)
        betas_ref[at] = upper
        return upper, inverse

    def orthonormalize(inverse):
        for p in range(pieces):
            current_ref[p] = plain_dot(inverse, residual_ref[p])

    own_lanes = pl.ds(pl.multiple_of(col * half, half), half)
    own_piece = row * n_sub + sub
    root_own = root_ref[own_piece]
    for iteration in range(alphas_ref.shape[0]):
        highs, lows = [], []
        for p in range(pieces):
            high, low = split_two(residual_ref[p, :, own_lanes] * root_ref[p, :, own_lanes])
            highs.append(high)
            lows.append(low)
        high = jnp.concatenate(highs, axis=1)
        both = jnp.concatenate([high, jnp.concatenate(lows, axis=1)], axis=0)
        first = lax.dot_general(both, tile_high[...], LAST, preferred_element_type=jnp.float32)
        second = lax.dot_general(high, tile_low[...], LAST, preferred_element_type=jnp.float32)
        halves = theirs_buf.at[iteration]
        halves[col] = first[:width] + (first[width:] + second)
        for step in range(1, n_col):
            peer = lax.rem(col + step, n_col)
            push(
                remote(
                    halves, col, half_send.at[iteration, step], half_recv.at[iteration, col],
                    {"col": peer},
                )
            )
        upper, inverse = factorize_residual(iteration)
        for step in range(1, n_col):
            peer = lax.rem(col + step, n_col)
            remote(
                halves, peer, half_send.at[iteration, step], half_recv.at[iteration, peer],
                {"col": peer},
            ).wait_recv()
        total = halves[0]
        for c in range(1, n_col):
            total = total + halves[c]
        got = piece_buf.at[iteration]
        got[own_piece] = total * root_own
        for step in range(1, n_row):
            peer = lax.rem(row + step, n_row)
            push(
                remote(
                    got, own_piece, piece_send.at[iteration, step],
                    piece_recv.at[iteration, row], {"row": peer},
                )
            )
        for hop in range(1, n_sub):
            to = lax.rem(sub + hop, n_sub)
            push(
                remote(
                    got, own_piece, piece_pass.at[iteration, 0, hop],
                    piece_took.at[iteration, row, sub], {"sub": to},
                )
            )
        if iteration > 0:
            for p in range(pieces):
                previous_ref[p] = current_ref[p]
        orthonormalize(inverse)
        for step in range(n_row - 1, 0, -1):
            peer = lax.rem(row + step, n_row)
            index = peer * n_sub + sub
            remote(
                got, index, piece_send.at[iteration, step], piece_recv.at[iteration, peer],
                {"row": peer},
            ).wait_recv()
            for hop in range(1, n_sub):
                to = lax.rem(sub + hop, n_sub)
                push(
                    remote(
                        got, index, piece_pass.at[iteration, step, hop],
                        piece_took.at[iteration, peer, sub], {"sub": to},
                    )
                )
        for hop in range(1, n_sub):
            source = lax.rem(sub + hop, n_sub)
            for step in range(n_row):
                peer = lax.rem(row + step, n_row)
                remote(
                    got, peer * n_sub + source, piece_pass.at[iteration, step, hop],
                    piece_took.at[iteration, peer, source], {"sub": source},
                ).wait_recv()
        alpha = jnp.zeros((width, width), jnp.float32)
        for p in range(pieces):
            if iteration > 0:
                mixed = plain_dot(
                    jnp.concatenate([inverse, -upper], axis=1),
                    jnp.concatenate([got[p], previous_ref[p]], axis=0),
                )
            else:
                mixed = plain_dot(inverse, got[p])
            residual_ref[p] = mixed
            alpha = alpha + dot_last(current_ref[p], mixed)
        alphas_ref[iteration] = alpha
        turned = alpha.T
        for p in range(pieces):
            residual_ref[p] = residual_ref[p] - plain_dot(turned, current_ref[p])

    _, inverse = factorize_residual(alphas_ref.shape[0])
    rows_own = pl.ds(pl.multiple_of(sub * half_width, half_width), half_width)
    mine_buf[...] = inverse
    for s in range(n_sub):
        panel_ref[:, s * half : (s + 1) * half] = plain_dot(
            mine_buf[rows_own, :], residual_ref[row * n_sub + s, :, own_lanes]
        )
    for copy in sent:
        copy.wait_send()


def hand_out_kernel(*refs):
    count = len(refs) // 3
    sources, targets, held = refs[:count], refs[count : 2 * count], refs[2 * count : 3 * count]
    sem = refs[-1]
    inward = [
        pltpu.make_async_copy(source, here, sem.at[0, at])
        for at, (source, here) in enumerate(zip(sources, held))
    ]
    outward = [
        pltpu.make_async_copy(here, target, sem.at[1, at])
        for at, (here, target) in enumerate(zip(held, targets))
    ]
    for copy in inward:
        copy.start()
    for copy, onward in zip(inward, outward):
        copy.wait()
        onward.start()
    for copy in outward:
        copy.wait()


def hand_out(*arrays):
    in_hbm = pl.BlockSpec(memory_space=pltpu.HBM)
    return pl.pallas_call(
        hand_out_kernel,
        out_shape=tuple(jax.ShapeDtypeStruct(array.shape, array.dtype) for array in arrays),
        in_specs=[in_hbm] * len(arrays),
        out_specs=(in_hbm,) * len(arrays),
        scratch_shapes=[pltpu.VMEM(array.shape, array.dtype) for array in arrays]
        + [pltpu.SemaphoreType.DMA((2, len(arrays)))],
        compiler_params=pltpu.CompilerParams(vmem_limit_bytes=60 * 2**20),
    )(*arrays)


def dense_on_device(tiles, tile_rows, tile_cols, tile_counts, start_panel):
    n_row, n_col, n_sub = (lax.axis_size(name) for name in ("row", "col", "sub"))
    slots, side, _ = tiles.shape
    half_width = start_panel.shape[1]
    width = half_width * n_sub
    half = side // n_sub
    devices = n_row * n_col * n_sub
    chips = n_row * n_col
    pieces = n_row * n_sub
    span = n_col * half
    in_vmem = pl.BlockSpec(memory_space=pltpu.VMEM)
    f32 = jnp.float32
    dma = pltpu.SemaphoreType.DMA
    panel, alphas, betas = pl.pallas_call(
        functools.partial(lanczos_kernel, n_row, n_col, n_sub),
        out_shape=(
            jax.ShapeDtypeStruct((half_width, side), f32),
            jax.ShapeDtypeStruct((ITERS, width, width), f32),
            jax.ShapeDtypeStruct((ITERS + 1, width, width), f32),
        ),
        in_specs=[pl.BlockSpec(memory_space=pltpu.HBM)] * 5,
        out_specs=(in_vmem, in_vmem, in_vmem),
        scratch_shapes=[
            pltpu.SMEM(tile_rows.shape, jnp.int32),
            pltpu.SMEM(tile_cols.shape, jnp.int32),
            pltpu.SMEM(tile_counts.shape, jnp.int32),
            dma((4,)),
            pltpu.VMEM((slots, half, side), f32),
            pltpu.VMEM((span, slots // n_col * side), jnp.bfloat16),
            pltpu.VMEM((span, slots // n_col * side), jnp.bfloat16),
            pltpu.VMEM((devices, half_width, side), f32),
            pltpu.VMEM((devices, 1, span), f32),
            pltpu.VMEM((width, width), f32),
            pltpu.VMEM((ITERS, n_col, width, span), f32),
            pltpu.VMEM((ITERS, pieces, width, span), f32),
            pltpu.VMEM((pieces, 1, span), f32),
            pltpu.VMEM((pieces, width, span), f32),
            pltpu.VMEM((pieces, width, span), f32),
            pltpu.VMEM((pieces, width, span), f32),
            dma((slots,)),
            dma((devices,)),
            dma((devices,)),
            dma((chips,)),
            dma((chips,)),
            dma((chips, n_sub)),
            dma((chips, n_sub)),
            dma((ITERS, n_col)),
            dma((ITERS, n_col)),
            dma((ITERS, n_row)),
            dma((ITERS, n_row)),
            dma((ITERS, n_row, n_sub)),
            dma((ITERS, n_row, n_sub)),
        ],
        compiler_params=pltpu.CompilerParams(
            collective_id=0, has_side_effects=True, vmem_limit_bytes=60 * 2**20
        ),
    )(tile_rows, tile_cols, tile_counts, tiles, start_panel.T)
    panel, alphas, betas = hand_out(panel, alphas, betas)
    return panel.T, alphas, betas


def on_one_device(tiles, tile_rows, tile_cols, tile_counts, start_panel):
    tile_side = tiles.shape[1]
    one_block = start_panel.shape[0] == tile_side
    covered = tiles.shape[0] == lax.axis_size("row") * lax.axis_size("col")
    form = dense_on_device if one_block and covered else on_device
    return form(tiles, tile_rows, tile_cols, tile_counts, start_panel)


def solution(mesh):
    return jax.shard_map(
        on_one_device,
        mesh=mesh,
        in_specs=(
            P(("parts", "row", "col"), None, None),
            P(("parts", "row", "col")),
            P(("parts", "row", "col")),
            P(("parts", "row", "col")),
            P(("parts", "row", "col"), "sub"),
        ),
        out_specs=(
            P(("parts", "row", "col"), "sub"),
            P("parts", None, None),
            P("parts", None, None),
        ),
        check_vma=False,
    )
```
